128 devices in a mesh: fsdp: 8 (over y, core), mat: 16 (over z, x).
Axes of the slice: x: 4, y: 4, z: 4, core: 2. Of those that a mesh axis runs over, the one named last changes fastest.
Arguments:
- momentum: float32 [8, 2048, 7168], P(None, 'mat', 'fsdp'), may hold values from -24 to 24
- gradient: bfloat16 [8, 2048, 7168], P(None, 'mat', 'fsdp')
Outputs:
- new_momentum: float32 [8, 2048, 7168], P(None, 'mat', 'fsdp')
- update: bfloat16 [8, 2048, 7168], P(None, 'mat', 'fsdp')
The draws below stay inside these ranges and needn't reach their ends.
All inputs are finite; a program needn't handle non-finite values.
Results may differ from the reference program's by a relative error of at most 0.015.
Values may be sent and summed in bfloat16 or wider, within the bound.
No kernel may reach another device: no remote copies, remote signals or barrier semaphores. Data moves between devices by JAX's collectives and lax.ppermute only.
A program may use at most 128 MiB of HBM per device.

```python
import math
import jax
import jax.numpy as jnp
from jax import lax

ROWS = 2048
COLS = 7168
POWER = 3
EXPERTS = 8


def draw_gradient(key, part):
    key = jax.random.fold_in(key, 7)
    subkeys = jax.random.split(key, 3)
    row_rise = jnp.exp(math.log(3.0) * jnp.arange(ROWS).astype(jnp.float32) / ROWS)
    col_rise = jnp.exp(math.log(3.0) * jnp.arange(COLS).astype(jnp.float32) / COLS)
    col_spread = jnp.exp(jax.random.uniform(subkeys[2], (EXPERTS, 1, COLS), jnp.float32, 0.0, math.log(4.0)))
    row_spread = jnp.exp(jax.random.uniform(subkeys[1], (EXPERTS, ROWS, 1), jnp.float32, 0.0, math.log(3.5)))
    values_raw = jax.random.normal(subkeys[0], (EXPERTS, ROWS, COLS), jnp.float32)
    scaled = values_raw * row_rise[None, :, None] * col_rise[None, None, :] * row_spread * col_spread
    return scaled.astype(jnp.bfloat16)


def steps_of(stream_key, shape, cuts, least, top_value):
    factor_of = 1.0
    for dim, parts in cuts:
        heights = jax.random.uniform(jax.random.fold_in(jax.random.fold_in(stream_key, 6), dim), (parts,), jnp.float32, least / len(cuts), top_value / len(cuts))
        factor_of = factor_of * jnp.repeat(jnp.exp(heights), shape[dim] // parts).reshape((-1,) + (1,) * (len(shape) - 1 - dim))
    return factor_of


def noise(own_key, dims, spread, reach, cuts=(), dtype=jnp.bfloat16):
    loudness = steps_of(own_key, dims, cuts, -0.22, 0.18) if cuts else 1.0
    array = jax.random.normal(own_key, dims, jnp.float32) * spread * loudness
    return jnp.minimum(jnp.maximum(array, -reach), reach).astype(dtype)


def setup_inputs(seed: int = 0) -> dict:
    key_list = jax.random.split(jax.random.key(seed), 3)
    momentum = noise(key_list[0], (EXPERTS, ROWS, COLS), 4.0, 24.0, ((1, 16), (2, 8)), jnp.float32)
    gradient = draw_gradient(jax.random.fold_in(key_list[2], 71), 0)
    return dict(momentum=momentum, gradient=gradient)


momentum_rate = 0.95
first_coef = 3.4445
second_coef = -4.775
third_coef = 2.0315
epsilon_value = 1e-06
highest = lax.Precision.HIGHEST

def per_expert(operands):
    previous, gradient_one = operands
    gradient_full = gradient_one.astype(jnp.float32)
    momentum_next = momentum_rate * previous + gradient_full
    blended = (gradient_full + momentum_rate * momentum_next).astype(jnp.bfloat16)
    raw_gram = lax.dot_general(blended, blended, (((1,), (1,)), ((), ())), preferred_element_type=jnp.float32)
    vector = jnp.ones((ROWS,), jnp.float32)
    for step_index in range(POWER):
        gram_image = jnp.dot(raw_gram, vector, precision=highest, preferred_element_type=jnp.float32)
        length = jnp.sqrt(jnp.sum(gram_image * gram_image) + epsilon_value)
        vector = gram_image / length
    scaling = lax.rsqrt(length + epsilon_value)
    started = (blended.astype(jnp.float32) * scaling).astype(jnp.bfloat16)
    gram_low = (raw_gram * (scaling * scaling)).astype(jnp.bfloat16)
    squared = jnp.dot(gram_low, gram_low, preferred_element_type=jnp.float32)
    poly_low = (second_coef * gram_low.astype(jnp.float32) + third_coef * squared).astype(jnp.bfloat16)
    product = jnp.dot(poly_low, started, preferred_element_type=jnp.float32)
    iterate = first_coef * started.astype(jnp.float32) + product
    return (momentum_next, (math.sqrt(COLS) * iterate).astype(jnp.bfloat16))

def reference(momentum, gradient):
    new_momentum, update = lax.map(per_expert, (momentum, gradient))
    return (new_momentum, update)
```

```python
import math

import jax
import jax.numpy as jnp
from jax import lax
from jax.experimental import pallas as pl
from jax.experimental.pallas import tpu as pltpu
from jax.sharding import PartitionSpec as P

EXPERTS, ROWS, COLS = 8, 2048, 7168
CORES, RING, PAIR = 2, 4, 2
MEMBERS = 16
LANES = ROWS // MEMBERS
WIDE = COLS // 8
HALF = WIDE // 2
BLOCK = 256
FOLD = 9 * BLOCK
PIECE = 128

momentum_rate = 0.95
first_coef = 3.4445
second_coef = -4.775
third_coef = 2.0315
epsilon_value = 1e-06
f32, bf16 = jnp.float32, jnp.bfloat16
PARAMS = pltpu.CompilerParams(vmem_limit_bytes=50 * 1024 * 1024)
WHOLE = pl.BlockSpec(memory_space=pltpu.VMEM)
SCALARS = pl.BlockSpec(memory_space=pltpu.SMEM)


def blend_kernel(momentum_ref, gradient_ref, new_ref, blended_ref):
    gradient = gradient_ref[0].astype(f32)
    new = momentum_rate * momentum_ref[0] + gradient
    new_ref[0] = new
    blended_ref[0] = (gradient + momentum_rate * new).astype(bf16).T


def blend(momentum, gradient):
    block = pl.BlockSpec((1, LANES, WIDE), lambda e: (e, 0, 0))
    return pl.pallas_call(
        blend_kernel,
        grid=(EXPERTS,),
        in_specs=[block, block],
        out_specs=[block, pl.BlockSpec((1, WIDE, LANES), lambda e: (e, 0, 0))],
        out_shape=[
            jax.ShapeDtypeStruct((EXPERTS, LANES, WIDE), f32),
            jax.ShapeDtypeStruct((EXPERTS, WIDE, LANES), bf16),
        ],
        compiler_params=PARAMS,
    )(momentum, gradient)


def place(half, piece, block):
    folded = 2 * half + piece // 2
    upper = block < 8 - folded
    row = jnp.where(upper, folded, 7 - folded) * BLOCK + (piece % 2) * PIECE
    column = jnp.where(upper, folded + block, block - 1) * BLOCK
    return pl.multiple_of(row, PIECE), pl.multiple_of(column, BLOCK)


def gram_kernel(where_ref, columns_ref, *piece_refs):
    half = where_ref[0]
    for slot, piece_ref in enumerate(piece_refs):
        piece = where_ref[1 + slot]
        folded = 2 * half + piece // 2
        top = columns_ref[2 * folded + piece % 2].T
        low = columns_ref[2 * (7 - folded) + piece % 2].T
        for block in range(9):
            _, column = place(half, piece, block)
            member = column // LANES
            right = jnp.concatenate([columns_ref[member], columns_ref[member + 1]], axis=1)
            left = jnp.where(block < 8 - folded, top, low) if 4 < block < 8 else (top if block <= 4 else low)
            piece_ref[:, block * BLOCK : (block + 1) * BLOCK] = jnp.dot(
                left, right, preferred_element_type=f32
            ).astype(bf16)


def gram_pieces(columns, half, pieces):
    where = jnp.stack([half, *pieces]).astype(jnp.int32)
    return pl.pallas_call(
        gram_kernel,
        in_specs=[SCALARS, WHOLE],
        out_specs=[WHOLE] * len(pieces),
        out_shape=[jax.ShapeDtypeStruct((PIECE, FOLD), bf16)] * len(pieces),
        compiler_params=PARAMS,
        cost_estimate=pl.CostEstimate(flops=2 * 2 * len(pieces) * PIECE * FOLD * 512, bytes_accessed=8_000_000, transcendentals=0),
    )(where, columns)


STEP = 16


def step_kernel(where_ref, columns_ref, *refs):
    piece_refs, out_ref = refs[: CORES * RING], refs[CORES * RING]
    gram, blended, mixed, image = refs[CORES * RING + 1 :]
    for slot, piece_ref in enumerate(piece_refs):
        half, piece = where_ref[2 * slot], where_ref[2 * slot + 1]
        for block in range(9):
            row, column = place(half, piece, block)
            values = piece_ref[:, block * BLOCK : (block + 1) * BLOCK]
            gram[pl.ds(row, PIECE), pl.ds(column, BLOCK)] = values
            gram[pl.ds(column, BLOCK), pl.ds(row, PIECE)] = values.T
    for member in range(MEMBERS):
        blended[:, member * LANES : (member + 1) * LANES] = columns_ref[member]

    def rows_of(step):
        return pl.ds(pl.multiple_of(step * STEP, STEP), STEP)

    def add_rows(step, total):
        return total + gram[rows_of(step), :].astype(f32)

    steps = ROWS // STEP
    total = lax.fori_loop(0, steps, add_rows, jnp.zeros((STEP, ROWS), f32))
    first = jnp.sum(total, axis=0, keepdims=True)
    first = first / jnp.sqrt(jnp.sum(first * first) + epsilon_value)

    def dot_rows(step, squares):
        values = jnp.sum(gram[rows_of(step), :].astype(f32) * first, axis=1, keepdims=True)
        image[rows_of(step), :] = values
        return squares + values * values

    squares = lax.fori_loop(0, steps, dot_rows, jnp.zeros((STEP, 1), f32))
    length = jnp.sqrt(jnp.sum(squares) + epsilon_value)

    def weigh_rows(step, total):
        return total + gram[rows_of(step), :].astype(f32) * (image[rows_of(step), :] / length)

    total = lax.fori_loop(0, steps, weigh_rows, jnp.zeros((STEP, ROWS), f32))
    third = jnp.sum(total, axis=0, keepdims=True)
    length = jnp.sqrt(jnp.sum(third * third) + epsilon_value)
    scale = lax.rsqrt(jnp.full((1, 1), length + epsilon_value, f32))
    square = scale * scale

    for block in range(8):
        at = slice(block * BLOCK, (block + 1) * BLOCK)
        product = jnp.dot(blended[...], gram[:, at], preferred_element_type=f32)
        mixed[:, at] = (second_coef * blended[:, at].astype(f32) + (third_coef * square) * product).astype(bf16)
    for block in range(8):
        at = slice(block * BLOCK, (block + 1) * BLOCK)
        product = jnp.dot(mixed[...], gram[:, at], preferred_element_type=f32)
        update = (math.sqrt(COLS) * scale) * (first_coef * blended[:, at].astype(f32) + square * product)
        update = update.astype(bf16)
        out_ref[2 * block] = update[:, :LANES]
        out_ref[2 * block + 1] = update[:, LANES:]


def newton_step(columns, pieces, where):
    return pl.pallas_call(
        step_kernel,
        in_specs=[SCALARS, WHOLE] + [WHOLE] * len(pieces),
        out_specs=WHOLE,
        out_shape=jax.ShapeDtypeStruct((MEMBERS, HALF, LANES), bf16),
        scratch_shapes=[
            pltpu.VMEM((ROWS, ROWS), bf16),
            pltpu.VMEM((HALF, ROWS), bf16),
            pltpu.VMEM((HALF, ROWS), bf16),
            pltpu.VMEM((ROWS, 1), f32),
        ],
        compiler_params=PARAMS,
        cost_estimate=pl.CostEstimate(flops=4 * ROWS * ROWS * HALF, bytes_accessed=8_000_000, transcendentals=0),
    )(where, columns, *pieces)


def spread_kernel(update_ref, out_ref):
    out_ref[0] = update_ref[0].T


def spread(update):
    return pl.pallas_call(
        spread_kernel,
        grid=(EXPERTS,),
        in_specs=[pl.BlockSpec((1, WIDE, LANES), lambda e: (e, 0, 0))],
        out_specs=pl.BlockSpec((1, LANES, WIDE), lambda e: (e, 0, 0)),
        out_shape=jax.ShapeDtypeStruct((EXPERTS, LANES, WIDE), bf16),
        compiler_params=PARAMS,
    )(update)


def add(*terms):
    total = terms[0].astype(f32)
    for term in terms[1:]:
        total = total + term.astype(f32)
    return total.astype(bf16)


def swap_cores(values):
    return lax.ppermute(values, "fsdp", [(i, i ^ 1) for i in range(CORES * RING)])


def shift(values, distance):
    size = CORES * RING
    return lax.ppermute(values, "fsdp", [(i, (i + CORES * distance) % size) for i in range(size)])


def swap_pair(values):
    return lax.ppermute(values, "mat", [(i, i ^ 1) for i in range(MEMBERS)])


def shards(momentum, gradient):
    index = lax.axis_index("fsdp")
    core, place_y = index % CORES, index // CORES
    order = (2, 1, 3, 0)
    new_momentum, blended = blend(momentum, gradient)
    columns = lax.all_to_all(blended.reshape(MEMBERS, HALF, LANES), "mat", 0, 0)

    wanted = [(place_y + distance) % RING for distance in order]
    away = gram_pieces(columns, 1 - core, wanted)
    kept = gram_pieces(columns, core, wanted)
    summed = [add(mine, swap_cores(theirs)) for mine, theirs in zip(kept, away)]
    arrived = [shift(values, distance) for values, distance in zip(summed, order) if distance]
    part = add(summed[-1], *arrived)
    total = add(part, swap_pair(part))

    own = [total] + [shift(total, distance) for distance in (1, 2, 3)]
    other = [swap_cores(values) for values in own]
    where = []
    for half in (core, 1 - core):
        for distance in range(RING):
            where += [half, (place_y - distance) % RING]
    update = newton_step(columns, own + other, jnp.stack(where).astype(jnp.int32))
    returned = lax.all_to_all(update, "mat", 0, 0)
    return new_momentum, spread(returned.reshape(EXPERTS, WIDE, LANES))


def solution(mesh):
    spec = P(None, "mat", "fsdp")
    return jax.shard_map(shards, mesh=mesh, in_specs=(spec, spec), out_specs=(spec, spec), check_vma=False)
```

```python
import functools
import math

import jax
import jax.numpy as jnp
from jax import lax
from jax.experimental import pallas as pl
from jax.experimental.pallas import tpu as pltpu
from jax.sharding import PartitionSpec as P

EXPERTS, ROWS, COLS = 8, 2048, 7168
CORES, RING, PAIR = 2, 4, 2
MEMBERS = 16
LANES = ROWS // MEMBERS
WIDE = COLS // 8
HALF = WIDE // 2
BLOCK = 256
FOLD = 9 * BLOCK
PIECE = 128

momentum_rate = 0.95
first_coef = 3.4445
second_coef = -4.775
third_coef = 2.0315
epsilon_value = 1e-06
f32, bf16 = jnp.float32, jnp.bfloat16
HALVES = PIECE // PAIR
PARAMS = pltpu.CompilerParams(vmem_limit_bytes=50 * 1024 * 1024)
WHOLE = pl.BlockSpec(memory_space=pltpu.VMEM)
ANYWHERE = pl.BlockSpec(memory_space=pl.ANY)
SCALARS = pl.BlockSpec(memory_space=pltpu.SMEM)


def blend_kernel(momentum_ref, gradient_ref, blended_ref):
    gradient = gradient_ref[0].astype(f32)
    new = momentum_rate * momentum_ref[0] + gradient
    blended_ref[0] = (gradient + momentum_rate * new).astype(bf16).T


def blend(momentum, gradient):
    block = pl.BlockSpec((1, LANES, WIDE), lambda e: (e, 0, 0))
    return pl.pallas_call(
        blend_kernel,
        grid=(EXPERTS,),
        in_specs=[block, block],
        out_specs=pl.BlockSpec((1, WIDE, LANES), lambda e: (e, 0, 0)),
        out_shape=jax.ShapeDtypeStruct((EXPERTS, WIDE, LANES), bf16),
        compiler_params=PARAMS,
    )(momentum, gradient)


def gram_kernel(groups, where_ref, columns_ref, *group_refs):
    half = where_ref[0]
    slot = 0
    for count, group_ref in zip(groups, group_refs):
        for member_slot in range(count):
            slot += 1
            piece = where_ref[slot]
            folded = 2 * half + piece // 2
            top = columns_ref[2 * folded + piece % 2].T
            low = columns_ref[2 * (7 - folded) + piece % 2].T
            for block in range(9):
                member = 2 * jnp.where(block < 8 - folded, folded + block, block - 1)
                right = jnp.concatenate([columns_ref[member], columns_ref[member + 1]], axis=1)
                left = jnp.where(block < 8 - folded, top, low) if 4 < block < 8 else (top if block <= 4 else low)
                values = jnp.dot(left, right, preferred_element_type=f32).astype(bf16)
                group_ref[member_slot, :, block * BLOCK : (block + 1) * BLOCK] = values


def gram_pieces(columns, half, groups, pieces):
    where = jnp.stack([half, *pieces]).astype(jnp.int32)
    return pl.pallas_call(
        functools.partial(gram_kernel, groups),
        in_specs=[SCALARS, WHOLE],
        out_specs=[WHOLE] * len(groups),
        out_shape=[jax.ShapeDtypeStruct((count, PIECE, FOLD), bf16) for count in groups],
        compiler_params=PARAMS,
        cost_estimate=pl.CostEstimate(
            flops=4 * len(pieces) * PIECE * FOLD * 512, bytes_accessed=2_000_000 * len(pieces), transcendentals=0
        ),
    )(where, columns)


STEP = 16


def step_kernel(layout, where_ref, columns_ref, *refs):
    piece_refs, out_ref = refs[: len(set(t[0] for t in layout))], refs[len(set(t[0] for t in layout))]
    parts, columns, staged, gram, blended, mixed, product, image, piece_sems, columns_sem, out_sems = refs[
        len(piece_refs) + 1 :
    ]
    copies = []
    for n, (array, start, rows) in enumerate(layout):
        target = parts.at[where_ref[2 * n], pl.ds(pl.multiple_of(where_ref[2 * n + 1], 32), rows), :]
        copies.append(pltpu.make_async_copy(piece_refs[array].at[pl.ds(start, rows), :], target, piece_sems.at[n]))
    for copy in copies:
        copy.start()
    columns_copy = pltpu.make_async_copy(columns_ref, columns, columns_sem)
    columns_copy.start()
    for copy in copies:
        copy.wait()
    for chunk in range(CORES * RING):
        folded, shifted = chunk // 2, chunk % 2 * PIECE
        for block in range(9):
            upper = block < 8 - folded
            row = (folded if upper else 7 - folded) * BLOCK + shifted
            column = (folded + block if upper else block - 1) * BLOCK
            values = parts[chunk, :, block * BLOCK : (block + 1) * BLOCK]
            gram[row : row + PIECE, column : column + BLOCK] = values
            if row // BLOCK * BLOCK != column:
                gram[column : column + BLOCK, row : row + PIECE] = values.T
    columns_copy.wait()
    for member in range(MEMBERS):
        blended[:, member * LANES : (member + 1) * LANES] = columns[member]

    def image_of(weights, blocks):
        total = jnp.zeros((8, ROWS), f32)
        for step in range(ROWS // STEP):
            if step % 16 == 0 and step // 16 < len(blocks):
                at = slice(blocks[step // 16] * BLOCK, (blocks[step // 16] + 1) * BLOCK)
                product[:, at] = jnp.dot(blended[...], gram[:, at], preferred_element_type=f32)
            at = slice(step * STEP, (step + 1) * STEP)
            values = gram[at, :].astype(f32)
            if weights is not None:
                values = values * weights[at, :]
            total = total + (values[:8] + values[8:])
        return jnp.sum(total, axis=0, keepdims=True)

    def length_of(values):
        return jnp.sqrt(jnp.sum(values * values) + epsilon_value)

    def stand(values):
        for member in range(MEMBERS):
            at = slice(member * LANES, (member + 1) * LANES)
            image[at, :] = jnp.broadcast_to(values[:, at], (8, LANES)).T[:, :1]

    values = image_of(None, (0, 1))
    stand(values / length_of(values))
    values = image_of(image, (2, 3, 4))
    stand(values / length_of(values))
    values = image_of(image, (5, 6, 7))
    scale = lax.rsqrt(jnp.full((1, 1), length_of(values) + epsilon_value, f32))
    square = scale * scale

    for block in range(8):
        at = slice(block * BLOCK, (block + 1) * BLOCK)
        mixed[:, at] = (second_coef * blended[:, at].astype(f32) + (third_coef * square) * product[:, at]).astype(bf16)
    out_copies = []
    for block in range(8):
        at = slice(block * BLOCK, (block + 1) * BLOCK)
        last = jnp.dot(mixed[...], gram[:, at], preferred_element_type=f32)
        update = (math.sqrt(COLS) * scale) * (first_coef * blended[:, at].astype(f32) + square * last)
        update = update.astype(bf16)
        staged[2 * block] = update[:, :LANES]
        staged[2 * block + 1] = update[:, LANES:]
        at = pl.ds(2 * block, 2)
        out_copies.append(pltpu.make_async_copy(staged.at[at], out_ref.at[at], out_sems.at[block]))
        out_copies[-1].start()
    for copy in out_copies:
        copy.wait()


def newton_step(columns, pieces, layout, where):
    matrix = (MEMBERS, HALF, LANES)
    return pl.pallas_call(
        functools.partial(step_kernel, layout),
        in_specs=[SCALARS, ANYWHERE] + [ANYWHERE] * len(pieces),
        out_specs=ANYWHERE,
        out_shape=jax.ShapeDtypeStruct(matrix, bf16),
        scratch_shapes=[
            pltpu.VMEM((CORES * RING, PIECE, FOLD), bf16),
            pltpu.VMEM(matrix, bf16),
            pltpu.VMEM(matrix, bf16),
            pltpu.VMEM((ROWS, ROWS), bf16),
            pltpu.VMEM((HALF, ROWS), bf16),
            pltpu.VMEM((HALF, ROWS), bf16),
            pltpu.VMEM((HALF, ROWS), f32),
            pltpu.VMEM((ROWS, 1), f32),
            pltpu.SemaphoreType.DMA((len(layout),)),
            pltpu.SemaphoreType.DMA,
            pltpu.SemaphoreType.DMA((8,)),
        ],
        compiler_params=PARAMS,
        cost_estimate=pl.CostEstimate(flops=4 * ROWS * ROWS * HALF, bytes_accessed=8_000_000, transcendentals=0),
    )(where, columns, *pieces)


def spread_kernel(update_ref, out_ref):
    out_ref[0] = update_ref[0].T


def spread(update):
    return pl.pallas_call(
        spread_kernel,
        grid=(EXPERTS,),
        in_specs=[pl.BlockSpec((1, WIDE, LANES), lambda e: (e, 0, 0))],
        out_specs=pl.BlockSpec((1, LANES, WIDE), lambda e: (e, 0, 0)),
        out_shape=jax.ShapeDtypeStruct((EXPERTS, LANES, WIDE), bf16),
        compiler_params=PARAMS,
    )(update)


def total_of(*terms):
    total = terms[0].astype(f32)
    for term in terms[1:]:
        total = total + term.astype(f32)
    return total


def add(*terms):
    return total_of(*terms).astype(bf16)


def swap_cores(values):
    return lax.ppermute(values, "fsdp", [(i, i ^ 1) for i in range(CORES * RING)])


def shift(values, distance):
    size = CORES * RING
    return lax.ppermute(values, "fsdp", [(i, (i + CORES * distance) % size) for i in range(size)])


def swap_pair(values):
    return lax.ppermute(values, "mat", [(i, i ^ 1) for i in range(MEMBERS)])


def shards(momentum, gradient):
    index = lax.axis_index("fsdp")
    core, place_y = index % CORES, index // CORES
    side = lax.axis_index("mat") % PAIR
    blended = blend(momentum, gradient)
    columns = lax.all_to_all(blended.reshape(MEMBERS, HALF, LANES), "mat", 0, 0)
    new_momentum = momentum_rate * momentum + gradient.astype(f32)

    far, ahead, behind = [(place_y + distance) % RING for distance in (2, 1, 3)]
    (away_far,) = gram_pieces(columns, 1 - core, (1,), [far])
    away_near, away_own = gram_pieces(columns, 1 - core, (2, 1), [ahead, behind, place_y])
    kept_far, kept_near, kept_own = gram_pieces(columns, core, (1, 2, 1), [far, ahead, behind, place_y])
    got_far = swap_cores(away_far)
    got_near = swap_cores(away_near)
    got_own = swap_cores(away_own)
    first, second = slice(0, HALVES), slice(HALVES, PIECE)
    via_behind = shift(add(kept_far[0, first], got_far[0, first]), 1)
    via_ahead = shift(add(kept_far[0, second], got_far[0, second]), -1)
    second_behind = shift(add(kept_near[0, second], got_near[0, second]), 1)
    first_ahead = shift(add(kept_near[1, first], got_near[1, first]), -1)
    first_behind = shift(add(kept_near[0, first], got_near[0, first], via_behind), 1)
    second_ahead = shift(add(kept_near[1, second], got_near[1, second], via_ahead), -1)
    first_sum = total_of(kept_own[0, first], got_own[0, first], first_ahead, first_behind)
    second_sum = total_of(kept_own[0, second], got_own[0, second], second_behind, second_ahead)
    given = jnp.where(side == 0, second_sum, first_sum).astype(bf16)
    own = add(jnp.where(side == 0, first_sum, second_sum), swap_pair(given))

    pieces, layout, where = [], [], []

    def take(array, *spans):
        swapped = swap_cores(array)
        for values, half in ((array, core), (swapped, 1 - core)):
            start = 0
            for rows, chunk, offset in spans:
                layout.append((len(pieces), start, rows))
                where.extend([half * RING + chunk, offset])
                start += rows
            pieces.append(values)

    opposite = swap_pair(own)
    quarter = HALVES // 2
    offsets = (side * HALVES, (1 - side) * HALVES)
    ends = []
    for half_piece, offset in zip((own, opposite), offsets):
        from_behind, from_ahead = shift(half_piece, 1), shift(half_piece, -1)
        take(half_piece, (HALVES, place_y, offset))
        take(from_behind, (HALVES, behind, offset))
        take(from_ahead, (HALVES, ahead, offset))
        ends += [shift(from_behind[:quarter], 1), shift(from_ahead[quarter:], -1)]
    spans = [(quarter, far, offset + part) for offset in offsets for part in (0, quarter)]
    take(jnp.concatenate(ends, axis=0), *spans)

    update = newton_step(columns, pieces, tuple(layout), jnp.stack(where).astype(jnp.int32))
    returned = lax.all_to_all(update, "mat", 0, 0)
    return new_momentum, spread(returned.reshape(EXPERTS, WIDE, LANES))


def solution(mesh):
    spec = P(None, "mat", "fsdp")
    return jax.shard_map(shards, mesh=mesh, in_specs=(spec, spec), out_specs=(spec, spec), check_vma=False)
```

```python
import functools
import math

import jax
import jax.numpy as jnp
from jax import lax
from jax.experimental import pallas as pl
from jax.experimental.pallas import tpu as pltpu
from jax.sharding import PartitionSpec as P

EXPERTS, ROWS, COLS = 8, 2048, 7168
CORES, RING, PAIR = 2, 4, 2
MEMBERS = 16
LANES = ROWS // MEMBERS
WIDE = COLS // 8
HALF = WIDE // 2
BLOCK = 256
TILES = ROWS // LANES
PIECE = LANES
FOLD = (TILES + 1) * LANES
HALVES = PIECE // PAIR
QUARTER = HALVES // PAIR

momentum_rate = 0.95
first_coef = 3.4445
second_coef = -4.775
third_coef = 2.0315
epsilon_value = 1e-06
f32, bf16 = jnp.float32, jnp.bfloat16
PARAMS = pltpu.CompilerParams(vmem_limit_bytes=50 * 1024 * 1024)
ALL_VMEM = pltpu.CompilerParams(vmem_limit_bytes=60 * 1024 * 1024)
WHOLE = pl.BlockSpec(memory_space=pltpu.VMEM)
ANYWHERE = pl.BlockSpec(memory_space=pl.ANY)
SCALARS = pl.BlockSpec(memory_space=pltpu.SMEM)


def blend_kernel(momentum_ref, gradient_ref, out_ref, momentum, gradient, blended, sems):
    copies = []
    for expert in range(EXPERTS):
        copies.append(pltpu.make_async_copy(momentum_ref.at[expert], momentum.at[expert], sems.at[0, expert]))
        copies.append(pltpu.make_async_copy(gradient_ref.at[expert], gradient.at[expert], sems.at[1, expert]))
    for copy in copies:
        copy.start()
    out_copies = []
    for expert in range(EXPERTS):
        copies[2 * expert].wait()
        copies[2 * expert + 1].wait()
        values = gradient[expert].astype(f32)
        new = momentum_rate * momentum[expert] + values
        blended[expert] = (values + momentum_rate * new).astype(bf16).T
        out_copies.append(pltpu.make_async_copy(blended.at[expert], out_ref.at[expert], sems.at[2, expert]))
        out_copies[-1].start()
    for copy in out_copies:
        copy.wait()


def blend(momentum, gradient):
    return pl.pallas_call(
        blend_kernel,
        in_specs=[ANYWHERE, ANYWHERE],
        out_specs=ANYWHERE,
        out_shape=jax.ShapeDtypeStruct((EXPERTS, WIDE, LANES), bf16),
        scratch_shapes=[
            pltpu.VMEM((EXPERTS, LANES, WIDE), f32),
            pltpu.VMEM((EXPERTS, LANES, WIDE), bf16),
            pltpu.VMEM((EXPERTS, WIDE, LANES), bf16),
            pltpu.SemaphoreType.DMA((3, EXPERTS)),
        ],
        compiler_params=ALL_VMEM,
    )(momentum, gradient)


def gram_kernel(where_ref, columns_ref, ring_ref, give_ref, keep_ref):
    half, side = where_ref[0], where_ref[1]
    for slot in range(RING):
        row = RING * half + where_ref[2 + slot]
        odd = row % 2
        count = (TILES - row) // 2
        top, low = columns_ref[row].T, columns_ref[TILES - 1 - row].T

        def put(left, right, at):
            values = jnp.dot(left, right, preferred_element_type=f32).astype(bf16)
            upper, lower = values[HALVES : HALVES + QUARTER], values[HALVES + QUARTER :]
            at = pl.ds(pl.multiple_of(at * LANES, LANES), values.shape[1])
            ring_ref[slot, :, at] = values[:HALVES]
            give_ref[slot, :, at] = jnp.where(side == 0, lower, upper)
            keep_ref[slot, :, at] = jnp.where(side == 0, upper, lower)

        on_top = odd == 1
        put(jnp.where(on_top, top, low), columns_ref[jnp.where(on_top, row, TILES - 1 - row)], jnp.where(on_top, 0, TILES - row))
        for block in range(TILES // 2):
            upper = block < count
            over = TILES - row - odd + 2 * (block - count)
            column = jnp.where(upper, row + odd + 2 * block, over)
            left = top if block < RING else jnp.where(upper, top, low)
            right = jnp.concatenate([columns_ref[column], columns_ref[column + 1]], axis=1)
            put(left, right, jnp.where(upper, odd + 2 * block, over + 1))


def gram_pieces(columns, half, side, pieces):
    where = jnp.stack([half, side, *pieces]).astype(jnp.int32)
    shapes = [(RING, HALVES, FOLD), (RING, QUARTER, FOLD), (RING, QUARTER, FOLD)]
    return pl.pallas_call(
        gram_kernel,
        in_specs=[SCALARS, WHOLE],
        out_specs=[WHOLE] * 3,
        out_shape=[jax.ShapeDtypeStruct(shape, bf16) for shape in shapes],
        compiler_params=PARAMS,
        cost_estimate=pl.CostEstimate(flops=16 * PIECE * FOLD * 512, bytes_accessed=8_000_000, transcendentals=0),
    )(where, columns)


def merge_kernel(where_ref, *refs):
    piece_refs, out_ref = refs[:-1], refs[-1]
    for n, piece_ref in enumerate(piece_refs):
        at = pl.ds(pl.multiple_of(where_ref[n], QUARTER), QUARTER)
        out_ref[at, :] = piece_ref[...]


def merge(pieces, offsets):
    count = len(pieces)
    return pl.pallas_call(
        merge_kernel,
        in_specs=[SCALARS] + [WHOLE] * count,
        out_specs=WHOLE,
        out_shape=jax.ShapeDtypeStruct((count * QUARTER, FOLD), bf16),
        compiler_params=PARAMS,
    )(jnp.stack([jnp.int32(offset) for offset in offsets]), *pieces)


STEP = 16


def step_kernel(layout, where_ref, columns_ref, *refs):
    count = 1 + max(array for array, _, _ in layout)
    piece_refs, out_ref, scratch = refs[:count], refs[count], refs[count + 1 :]
    parts, staged, gram, blended, mixed, product, image, out_sems = scratch
    for n, (array, start, rows) in enumerate(layout):
        at = pl.ds(pl.multiple_of(where_ref[2 * n + 1], QUARTER), rows)
        parts[where_ref[2 * n], at, :] = piece_refs[array][start : start + rows, :]
    for folded in range(TILES // 2):
        for row, start in ((folded, 0), (TILES - 1 - folded, TILES - folded)):
            at = slice(row * LANES, (row + 1) * LANES)
            gram[at, row * LANES :] = parts[folded, :, start * LANES : (start + TILES - row) * LANES]
            for column in range(row + 1, TILES, 2):
                wide = min(2, TILES - column) * LANES
                begin = (start + column - row) * LANES
                gram[column * LANES : column * LANES + wide, at] = parts[folded, :, begin : begin + wide].T
    for member in range(MEMBERS):
        blended[:, member * LANES : (member + 1) * LANES] = columns_ref[member]

    def image_of(weights, blocks):
        total = jnp.zeros((8, ROWS), f32)
        for step in range(ROWS // STEP):
            if step % 16 == 0 and step // 16 < len(blocks):
                at = slice(blocks[step // 16] * BLOCK, (blocks[step // 16] + 1) * BLOCK)
                product[:, at] = jnp.dot(blended[...], gram[:, at], preferred_element_type=f32)
            at = slice(step * STEP, (step + 1) * STEP)
            values = gram[at, :].astype(f32)
            if weights is not None:
                values = values * weights[at, :]
            total = total + (values[:8] + values[8:])
        return jnp.sum(total, axis=0, keepdims=True)

    def length_of(values):
        return jnp.sqrt(jnp.sum(values * values) + epsilon_value)

    def stand(values):
        for member in range(MEMBERS):
            at = slice(member * LANES, (member + 1) * LANES)
            image[at, :] = jnp.broadcast_to(values[:, at], (8, LANES)).T[:, :1]

    values = image_of(None, (0, 1))
    stand(values / length_of(values))
    values = image_of(image, (2, 3, 4))
    stand(values / length_of(values))
    values = image_of(image, (5, 6, 7))
    scale = lax.rsqrt(jnp.full((1, 1), length_of(values) + epsilon_value, f32))
    square = scale * scale

    for block in range(8):
        at = slice(block * BLOCK, (block + 1) * BLOCK)
        mixed[:, at] = (second_coef * blended[:, at].astype(f32) + (third_coef * square) * product[:, at]).astype(bf16)
    out_copies = []
    for block in range(8):
        at = slice(block * BLOCK, (block + 1) * BLOCK)
        last = jnp.dot(mixed[...], gram[:, at], preferred_element_type=f32)
        update = (math.sqrt(COLS) * scale) * (first_coef * blended[:, at].astype(f32) + square * last)
        update = update.astype(bf16)
        staged[2 * block] = update[:, :LANES]
        staged[2 * block + 1] = update[:, LANES:]
        at = pl.ds(2 * block, 2)
        out_copies.append(pltpu.make_async_copy(staged.at[at], out_ref.at[at], out_sems.at[block]))
        out_copies[-1].start()
    for copy in out_copies:
        copy.wait()


def newton_step(columns, pieces, layout, where):
    matrix = (MEMBERS, HALF, LANES)
    return pl.pallas_call(
        functools.partial(step_kernel, layout),
        in_specs=[SCALARS, WHOLE] + [WHOLE] * len(pieces),
        out_specs=ANYWHERE,
        out_shape=jax.ShapeDtypeStruct(matrix, bf16),
        scratch_shapes=[
            pltpu.VMEM((CORES * RING, PIECE, FOLD), bf16),
            pltpu.VMEM(matrix, bf16),
            pltpu.VMEM((ROWS, ROWS), bf16),
            pltpu.VMEM((HALF, ROWS), bf16),
            pltpu.VMEM((HALF, ROWS), bf16),
            pltpu.VMEM((HALF, ROWS), f32),
            pltpu.VMEM((ROWS, 1), f32),
            pltpu.SemaphoreType.DMA((8,)),
        ],
        compiler_params=PARAMS,
        cost_estimate=pl.CostEstimate(flops=4 * ROWS * ROWS * HALF, bytes_accessed=8_000_000, transcendentals=0),
    )(where, columns, *pieces)


def spread_kernel(update_ref, out_ref, turned, sems):
    out_copies = []
    for expert in range(EXPERTS):
        turned[expert] = update_ref[expert].T
        out_copies.append(pltpu.make_async_copy(turned.at[expert], out_ref.at[expert], sems.at[expert]))
        out_copies[-1].start()
    for copy in out_copies:
        copy.wait()


def spread(update):
    return pl.pallas_call(
        spread_kernel,
        in_specs=[WHOLE],
        out_specs=ANYWHERE,
        out_shape=jax.ShapeDtypeStruct((EXPERTS, LANES, WIDE), bf16),
        scratch_shapes=[pltpu.VMEM((EXPERTS, LANES, WIDE), bf16), pltpu.SemaphoreType.DMA((EXPERTS,))],
        compiler_params=PARAMS,
    )(update)


def total_of(*terms):
    total = terms[0].astype(f32)
    for term in terms[1:]:
        total = total + term.astype(f32)
    return total


def add(*terms):
    return total_of(*terms).astype(bf16)


def swap_cores(values):
    return lax.ppermute(values, "fsdp", [(i, i ^ 1) for i in range(CORES * RING)])


def shift(values, distance):
    size = CORES * RING
    return lax.ppermute(values, "fsdp", [(i, (i + CORES * distance) % size) for i in range(size)])


def swap_pair(values):
    return lax.ppermute(values, "mat", [(i, i ^ 1) for i in range(MEMBERS)])


def shards(momentum, gradient):
    index = lax.axis_index("fsdp")
    core, place_y = index % CORES, index // CORES
    side = lax.axis_index("mat") % PAIR
    blended = blend(momentum, gradient)
    columns = lax.all_to_all(blended.reshape(MEMBERS, HALF, LANES), "mat", 0, 0)
    new_momentum = momentum_rate * momentum + gradient.astype(f32)

    far, ahead, behind = [(place_y + distance) % RING for distance in (2, 1, 3)]
    wanted = [far, ahead, behind, place_y]
    away = gram_pieces(columns, 1 - core, side, wanted)
    kept_ring, kept_give, kept_keep = gram_pieces(columns, core, side, wanted)
    got_give, got_ring, got_keep = swap_cores(away[1]), swap_cores(away[0]), swap_cores(away[2])

    def round_ring(pieces):
        return [shift(values, distance) for values, distance in zip(pieces, (2, 1, 3))]

    ring_sums = [add(kept_ring[slot], got_ring[slot]) for slot in range(3)]
    partner = swap_pair(add(kept_give, got_give))
    *arrived, partner = lax.optimization_barrier((*round_ring(ring_sums), partner))
    ring_total = total_of(kept_ring[3], got_ring[3], *arrived)
    upper, lower = ring_total[:QUARTER], ring_total[QUARTER:]
    partner_sums = [add(kept_keep[slot], got_keep[slot], partner[slot]) for slot in range(3)]
    upper_got = swap_pair(jnp.where(side == 0, lower, upper).astype(bf16))
    *arrived, upper_got = lax.optimization_barrier((*round_ring(partner_sums), upper_got))
    first = add(jnp.where(side == 0, upper, lower), upper_got)
    second = add(kept_keep[3], got_keep[3], partner[3], *arrived)

    first_other = swap_pair(first)
    *arrived, first_other = lax.optimization_barrier((*round_ring([second] * 3), first_other))
    first = merge((first, first_other), (side * QUARTER, (1 - side) * QUARTER))
    second = merge((second, *arrived), range(0, PIECE, QUARTER))
    second_other = swap_pair(second)
    pieces, layout, where = [], [], []

    def take(array, rows, chunks, offset):
        for values, half in ((array, core), (swap_cores(array), 1 - core)):
            for n, chunk in enumerate(chunks):
                layout.append((len(pieces), n * rows, rows))
                where.extend([half * RING + chunk, offset])
            pieces.append(values)

    order = [place_y, far, behind, ahead]
    take(first, HALVES, order[:1], 0)
    take(second, QUARTER, order, HALVES + side * QUARTER)
    for values, chunk in zip(round_ring([first] * 3), order[1:]):
        take(values, HALVES, [chunk], 0)
    take(second_other, QUARTER, order, HALVES + (1 - side) * QUARTER)

    update = newton_step(columns, pieces, tuple(layout), jnp.stack(where).astype(jnp.int32))
    returned = lax.all_to_all(update, "mat", 0, 0)
    return new_momentum, spread(returned.reshape(EXPERTS, WIDE, LANES))


def solution(mesh):
    spec = P(None, "mat", "fsdp")
    return jax.shard_map(shards, mesh=mesh, in_specs=(spec, spec), out_specs=(spec, spec), check_vma=False)
```

```python
import functools
import math

import jax
import jax.numpy as jnp
from jax import lax
from jax.experimental import pallas as pl
from jax.experimental.pallas import tpu as pltpu
from jax.sharding import PartitionSpec as P

EXPERTS, ROWS, COLS = 8, 2048, 7168
CORES, RING, PAIR = 2, 4, 2
MEMBERS = 16
LANES = ROWS // MEMBERS
WIDE = COLS // 8
HALF = WIDE // 2
BLOCK = 256
TILES = ROWS // LANES
PIECE = LANES
FOLD = (TILES + 1) * LANES
HALVES = PIECE // PAIR
QUARTER = HALVES // PAIR

momentum_rate = 0.95
first_coef = 3.4445
second_coef = -4.775
third_coef = 2.0315
epsilon_value = 1e-06
f32, bf16 = jnp.float32, jnp.bfloat16
PARAMS = pltpu.CompilerParams(vmem_limit_bytes=50 * 1024 * 1024)
ALL_VMEM = pltpu.CompilerParams(vmem_limit_bytes=60 * 1024 * 1024)
WHOLE = pl.BlockSpec(memory_space=pltpu.VMEM)
ANYWHERE = pl.BlockSpec(memory_space=pl.ANY)
SCALARS = pl.BlockSpec(memory_space=pltpu.SMEM)


def blend_kernel(momentum_ref, gradient_ref, out_ref, momentum, gradient, blended, sems):
    copies = []
    for expert in range(EXPERTS):
        copies.append(pltpu.make_async_copy(momentum_ref.at[expert], momentum.at[expert], sems.at[0, expert]))
        copies.append(pltpu.make_async_copy(gradient_ref.at[expert], gradient.at[expert], sems.at[1, expert]))
    for copy in copies:
        copy.start()
    out_copies = []
    for expert in range(EXPERTS):
        copies[2 * expert].wait()
        copies[2 * expert + 1].wait()
        values = gradient[expert].astype(f32)
        new = momentum_rate * momentum[expert] + values
        blended[expert] = (values + momentum_rate * new).astype(bf16).T
        out_copies.append(pltpu.make_async_copy(blended.at[expert], out_ref.at[expert], sems.at[2, expert]))
        out_copies[-1].start()
    for copy in out_copies:
        copy.wait()


def blend(momentum, gradient):
    return pl.pallas_call(
        blend_kernel,
        in_specs=[ANYWHERE, ANYWHERE],
        out_specs=ANYWHERE,
        out_shape=jax.ShapeDtypeStruct((EXPERTS, WIDE, LANES), bf16),
        scratch_shapes=[
            pltpu.VMEM((EXPERTS, LANES, WIDE), f32),
            pltpu.VMEM((EXPERTS, LANES, WIDE), bf16),
            pltpu.VMEM((EXPERTS, WIDE, LANES), bf16),
            pltpu.SemaphoreType.DMA((3, EXPERTS)),
        ],
        compiler_params=ALL_VMEM,
    )(momentum, gradient)


def gram_kernel(where_ref, columns_ref, ring_ref, give_ref, keep_ref, turned):
    side = where_ref[1]

    def half_of(half):
        folded = range(RING * half, RING * (half + 1))
        rows = sorted([*folded, *(TILES - 1 - row for row in folded)])
        for n, row in enumerate(rows):
            turned[n * LANES : (n + 1) * LANES, :] = columns_ref[row].T
        for column in range(0, TILES, 2):
            used = [row for row in rows if row <= column + 1]
            right = jnp.concatenate([columns_ref[column], columns_ref[column + 1]], axis=1)
            product = jnp.dot(turned[: len(used) * LANES, :], right, preferred_element_type=f32)
            for n, row in enumerate(used):
                begin = LANES if row > column else 0
                values = product[n * LANES : (n + 1) * LANES, begin:].astype(bf16)
                upper, lower = values[HALVES : HALVES + QUARTER], values[HALVES + QUARTER :]
                top = row in folded
                slot = where_ref[2 + (row if top else TILES - 1 - row) - RING * half]
                start = column * LANES + begin + (-row if top else 1) * LANES
                at = slice(start, start + values.shape[1])
                ring_ref[slot, :, at] = values[:HALVES]
                give_ref[slot, :, at] = jnp.where(side == 0, lower, upper)
                keep_ref[slot, :, at] = jnp.where(side == 0, upper, lower)

    for half in range(CORES):
        pl.when(where_ref[0] == half)(functools.partial(half_of, half))


def gram_pieces(columns, half, side, slots):
    where = jnp.concatenate([jnp.stack([half, side]), slots]).astype(jnp.int32)
    shapes = [(RING, HALVES, FOLD), (RING, QUARTER, FOLD), (RING, QUARTER, FOLD)]
    return pl.pallas_call(
        gram_kernel,
        in_specs=[SCALARS, WHOLE],
        out_specs=[WHOLE] * 3,
        out_shape=[jax.ShapeDtypeStruct(shape, bf16) for shape in shapes],
        scratch_shapes=[pltpu.VMEM((ROWS // CORES, HALF), bf16)],
        compiler_params=PARAMS,
        cost_estimate=pl.CostEstimate(flops=16 * PIECE * FOLD * 512, bytes_accessed=8_000_000, transcendentals=0),
    )(where, columns)


def merge_kernel(where_ref, *refs):
    piece_refs, out_ref = refs[:-1], refs[-1]
    for n, piece_ref in enumerate(piece_refs):
        at = pl.ds(pl.multiple_of(where_ref[n], QUARTER), QUARTER)
        out_ref[at, :] = piece_ref[...]


def merge(pieces, offsets):
    count = len(pieces)
    return pl.pallas_call(
        merge_kernel,
        in_specs=[SCALARS] + [WHOLE] * count,
        out_specs=WHOLE,
        out_shape=jax.ShapeDtypeStruct((count * QUARTER, FOLD), bf16),
        compiler_params=PARAMS,
    )(jnp.stack([jnp.int32(offset) for offset in offsets]), *pieces)


STEP = 16


def step_kernel(layout, where_ref, columns_ref, *refs):
    count = 1 + max(array for array, _, _ in layout)
    piece_refs, out_ref, scratch = refs[:count], refs[count], refs[count + 1 :]
    parts, staged, gram, blended, mixed, product, image, out_sems = scratch
    for n, (array, start, rows) in enumerate(layout):
        at = pl.ds(pl.multiple_of(where_ref[2 * n + 1], QUARTER), rows)
        parts[where_ref[2 * n], at, :] = piece_refs[array][start : start + rows, :]
    for folded in range(TILES // 2):
        for row, start in ((folded, 0), (TILES - 1 - folded, TILES - folded)):
            at = slice(row * LANES, (row + 1) * LANES)
            gram[at, row * LANES :] = parts[folded, :, start * LANES : (start + TILES - row) * LANES]
            for column in range(row + 1, TILES, 2):
                wide = min(2, TILES - column) * LANES
                begin = (start + column - row) * LANES
                gram[column * LANES : column * LANES + wide, at] = parts[folded, :, begin : begin + wide].T
    for member in range(MEMBERS):
        blended[:, member * LANES : (member + 1) * LANES] = columns_ref[member]

    def image_of(weights, blocks):
        total = jnp.zeros((8, ROWS), f32)
        for step in range(ROWS // STEP):
            if step % 16 == 0 and step // 16 < len(blocks):
                at = slice(blocks[step // 16] * BLOCK, (blocks[step // 16] + 1) * BLOCK)
                product[:, at] = jnp.dot(blended[...], gram[:, at], preferred_element_type=f32)
            at = slice(step * STEP, (step + 1) * STEP)
            values = gram[at, :].astype(f32)
            if weights is not None:
                values = values * weights[at, :]
            total = total + (values[:8] + values[8:])
        return jnp.sum(total, axis=0, keepdims=True)

    def length_of(values):
        return jnp.sqrt(jnp.sum(values * values) + epsilon_value)

    def stand(values):
        for member in range(MEMBERS):
            at = slice(member * LANES, (member + 1) * LANES)
            image[at, :] = jnp.broadcast_to(values[:, at], (8, LANES)).T[:, :1]

    values = image_of(None, (0, 1))
    stand(values / length_of(values))
    values = image_of(image, (2, 3, 4))
    stand(values / length_of(values))
    values = image_of(image, (5, 6, 7))
    scale = lax.rsqrt(jnp.full((1, 1), length_of(values) + epsilon_value, f32))
    square = scale * scale

    for block in range(8):
        at = slice(block * BLOCK, (block + 1) * BLOCK)
        mixed[:, at] = (second_coef * blended[:, at].astype(f32) + (third_coef * square) * product[:, at]).astype(bf16)
    out_copies = []
    for block in range(8):
        at = slice(block * BLOCK, (block + 1) * BLOCK)
        last = jnp.dot(mixed[...], gram[:, at], preferred_element_type=f32)
        update = (math.sqrt(COLS) * scale) * (first_coef * blended[:, at].astype(f32) + square * last)
        update = update.astype(bf16)
        staged[2 * block] = update[:, :LANES]
        staged[2 * block + 1] = update[:, LANES:]
        at = pl.ds(2 * block, 2)
        out_copies.append(pltpu.make_async_copy(staged.at[at], out_ref.at[at], out_sems.at[block]))
        out_copies[-1].start()
    for copy in out_copies:
        copy.wait()


def newton_step(columns, pieces, layout, where):
    matrix = (MEMBERS, HALF, LANES)
    return pl.pallas_call(
        functools.partial(step_kernel, layout),
        in_specs=[SCALARS, WHOLE] + [WHOLE] * len(pieces),
        out_specs=ANYWHERE,
        out_shape=jax.ShapeDtypeStruct(matrix, bf16),
        scratch_shapes=[
            pltpu.VMEM((CORES * RING, PIECE, FOLD), bf16),
            pltpu.VMEM(matrix, bf16),
            pltpu.VMEM((ROWS, ROWS), bf16),
            pltpu.VMEM((HALF, ROWS), bf16),
            pltpu.VMEM((HALF, ROWS), bf16),
            pltpu.VMEM((HALF, ROWS), f32),
            pltpu.VMEM((ROWS, 1), f32),
            pltpu.SemaphoreType.DMA((8,)),
        ],
        compiler_params=PARAMS,
        cost_estimate=pl.CostEstimate(flops=4 * ROWS * ROWS * HALF, bytes_accessed=8_000_000, transcendentals=0),
    )(where, columns, *pieces)


def spread_kernel(update_ref, out_ref, turned, sems):
    out_copies = []
    for expert in range(EXPERTS):
        turned[expert] = update_ref[expert].T
        out_copies.append(pltpu.make_async_copy(turned.at[expert], out_ref.at[expert], sems.at[expert]))
        out_copies[-1].start()
    for copy in out_copies:
        copy.wait()


def spread(update):
    return pl.pallas_call(
        spread_kernel,
        in_specs=[WHOLE],
        out_specs=ANYWHERE,
        out_shape=jax.ShapeDtypeStruct((EXPERTS, LANES, WIDE), bf16),
        scratch_shapes=[pltpu.VMEM((EXPERTS, LANES, WIDE), bf16), pltpu.SemaphoreType.DMA((EXPERTS,))],
        compiler_params=PARAMS,
    )(update)


def total_of(*terms):
    total = terms[0].astype(f32)
    for term in terms[1:]:
        total = total + term.astype(f32)
    return total


def add(*terms):
    return total_of(*terms).astype(bf16)


def swap_cores(values):
    return lax.ppermute(values, "fsdp", [(i, i ^ 1) for i in range(CORES * RING)])


def shift(values, distance):
    size = CORES * RING
    return lax.ppermute(values, "fsdp", [(i, (i + CORES * distance) % size) for i in range(size)])


def swap_pair(values):
    return lax.ppermute(values, "mat", [(i, i ^ 1) for i in range(MEMBERS)])


def shards(momentum, gradient):
    index = lax.axis_index("fsdp")
    core, place_y = index % CORES, index // CORES
    side = lax.axis_index("mat") % PAIR
    blended = blend(momentum, gradient)
    columns = lax.all_to_all(blended.reshape(MEMBERS, HALF, LANES), "mat", 0, 0)
    new_momentum = momentum_rate * momentum + gradient.astype(f32)

    far, ahead, behind = [(place_y + distance) % RING for distance in (2, 1, 3)]
    slots = jnp.array([3, 1, 0, 2])[(jnp.arange(RING) - place_y) % RING]
    away = gram_pieces(columns, 1 - core, side, slots)
    kept_ring, kept_give, kept_keep = gram_pieces(columns, core, side, slots)
    got_give, got_ring, got_keep = swap_cores(away[1]), swap_cores(away[0]), swap_cores(away[2])

    def round_ring(pieces):
        return [shift(values, distance) for values, distance in zip(pieces, (2, 1, 3))]

    ring_sums = [add(kept_ring[slot], got_ring[slot]) for slot in range(3)]
    partner = swap_pair(add(kept_give, got_give))
    *arrived, partner = lax.optimization_barrier((*round_ring(ring_sums), partner))
    first = add(kept_ring[3], got_ring[3], *arrived)
    partner_sums = [add(kept_keep[slot], got_keep[slot], partner[slot]) for slot in range(3)]
    first_got = swap_pair(first)
    *arrived, first_got = lax.optimization_barrier((*round_ring(partner_sums), first_got))
    first = add(first, first_got)
    second = add(kept_keep[3], got_keep[3], partner[3], *arrived)

    second = merge((second, *round_ring([second] * 3)), range(0, PIECE, QUARTER))
    second_other = swap_pair(second)
    pieces, layout, where = [], [], []

    def take(array, rows, chunks, offset):
        for values, half in ((array, core), (swap_cores(array), 1 - core)):
            for n, chunk in enumerate(chunks):
                layout.append((len(pieces), n * rows, rows))
                where.extend([half * RING + chunk, offset])
            pieces.append(values)

    order = [place_y, far, behind, ahead]
    take(first, HALVES, order[:1], 0)
    take(second, QUARTER, order, HALVES + side * QUARTER)
    for values, chunk in zip(round_ring([first] * 3), order[1:]):
        take(values, HALVES, [chunk], 0)
    take(second_other, QUARTER, order, HALVES + (1 - side) * QUARTER)

    update = newton_step(columns, pieces, tuple(layout), jnp.stack(where).astype(jnp.int32))
    returned = lax.all_to_all(update, "mat", 0, 0)
    return new_momentum, spread(returned.reshape(EXPERTS, WIDE, LANES))


def solution(mesh):
    spec = P(None, "mat", "fsdp")
    return jax.shard_map(shards, mesh=mesh, in_specs=(spec, spec), out_specs=(spec, spec), check_vma=False)
```

```python
import functools
import math

import jax
import jax.numpy as jnp
from jax import lax
from jax.experimental import pallas as pl
from jax.experimental.pallas import tpu as pltpu
from jax.sharding import PartitionSpec as P

EXPERTS, ROWS, COLS = 8, 2048, 7168
CORES, RING, PAIR = 2, 4, 2
MEMBERS = 16
LANES = ROWS // MEMBERS
WIDE = COLS // 8
HALF = WIDE // 2
BLOCK = 256
TILES = ROWS // LANES
PIECE = LANES
FOLD = (TILES + 1) * LANES
HALVES = PIECE // PAIR
QUARTER = HALVES // PAIR

momentum_rate = 0.95
first_coef = 3.4445
second_coef = -4.775
third_coef = 2.0315
epsilon_value = 1e-06
f32, bf16 = jnp.float32, jnp.bfloat16
PARAMS = pltpu.CompilerParams(vmem_limit_bytes=50 * 1024 * 1024)
ALL_VMEM = pltpu.CompilerParams(vmem_limit_bytes=60 * 1024 * 1024)
WHOLE = pl.BlockSpec(memory_space=pltpu.VMEM)
ANYWHERE = pl.BlockSpec(memory_space=pl.ANY)
SCALARS = pl.BlockSpec(memory_space=pltpu.SMEM)


def blend_kernel(momentum_ref, gradient_ref, out_ref, momentum, gradient, blended, sems):
    copies = []
    for expert in range(EXPERTS):
        copies.append(pltpu.make_async_copy(momentum_ref.at[expert], momentum.at[expert], sems.at[0, expert]))
        copies.append(pltpu.make_async_copy(gradient_ref.at[expert], gradient.at[expert], sems.at[1, expert]))
    for copy in copies:
        copy.start()
    out_copies = []
    for expert in range(EXPERTS):
        copies[2 * expert].wait()
        copies[2 * expert + 1].wait()
        values = gradient[expert].astype(f32)
        new = momentum_rate * momentum[expert] + values
        blended[expert] = (values + momentum_rate * new).astype(bf16).T
        out_copies.append(pltpu.make_async_copy(blended.at[expert], out_ref.at[expert], sems.at[2, expert]))
        out_copies[-1].start()
    for copy in out_copies:
        copy.wait()


def blend(momentum, gradient):
    return pl.pallas_call(
        blend_kernel,
        in_specs=[ANYWHERE, ANYWHERE],
        out_specs=ANYWHERE,
        out_shape=jax.ShapeDtypeStruct((EXPERTS, WIDE, LANES), bf16),
        scratch_shapes=[
            pltpu.VMEM((EXPERTS, LANES, WIDE), f32),
            pltpu.VMEM((EXPERTS, LANES, WIDE), bf16),
            pltpu.VMEM((EXPERTS, WIDE, LANES), bf16),
            pltpu.SemaphoreType.DMA((3, EXPERTS)),
        ],
        compiler_params=ALL_VMEM,
    )(momentum, gradient)


def gram_kernel(where_ref, columns_ref, ring_ref, give_ref, keep_ref, turned):
    side = where_ref[1]

    def half_of(half):
        folded = range(RING * half, RING * (half + 1))
        rows = sorted([*folded, *(TILES - 1 - row for row in folded)])
        for n, row in enumerate(rows):
            turned[n * LANES : (n + 1) * LANES, :] = columns_ref[row].T
        for column in range(0, TILES, 2):
            used = [row for row in rows if row <= column + 1]
            right = jnp.concatenate([columns_ref[column], columns_ref[column + 1]], axis=1)
            product = jnp.dot(turned[: len(used) * LANES, :], right, preferred_element_type=f32)
            for n, row in enumerate(used):
                begin = LANES if row > column else 0
                values = product[n * LANES : (n + 1) * LANES, begin:].astype(bf16)
                upper, lower = values[HALVES : HALVES + QUARTER], values[HALVES + QUARTER :]
                top = row in folded
                slot = where_ref[2 + (row if top else TILES - 1 - row) - RING * half]
                start = column * LANES + begin + (-row if top else 1) * LANES
                at = slice(start, start + values.shape[1])
                ring_ref[slot, :, at] = values[:HALVES]
                give_ref[slot, :, at] = jnp.where(side == 0, lower, upper)
                keep_ref[slot, :, at] = jnp.where(side == 0, upper, lower)

    for half in range(CORES):
        pl.when(where_ref[0] == half)(functools.partial(half_of, half))


def gram_pieces(columns, half, side, slots):
    where = jnp.concatenate([jnp.stack([half, side]), slots]).astype(jnp.int32)
    shapes = [(RING, HALVES, FOLD), (RING, QUARTER, FOLD), (RING, QUARTER, FOLD)]
    return pl.pallas_call(
        gram_kernel,
        in_specs=[SCALARS, WHOLE],
        out_specs=[WHOLE] * 3,
        out_shape=[jax.ShapeDtypeStruct(shape, bf16) for shape in shapes],
        scratch_shapes=[pltpu.VMEM((ROWS // CORES, HALF), bf16)],
        compiler_params=PARAMS,
        cost_estimate=pl.CostEstimate(flops=16 * PIECE * FOLD * 512, bytes_accessed=8_000_000, transcendentals=0),
    )(where, columns)


def merge_kernel(where_ref, *refs):
    piece_refs, out_ref = refs[:-1], refs[-1]
    for n, piece_ref in enumerate(piece_refs):
        at = pl.ds(pl.multiple_of(where_ref[n], QUARTER), QUARTER)
        out_ref[at, :] = piece_ref[...]


def merge(pieces, offsets):
    count = len(pieces)
    return pl.pallas_call(
        merge_kernel,
        in_specs=[SCALARS] + [WHOLE] * count,
        out_specs=WHOLE,
        out_shape=jax.ShapeDtypeStruct((count * QUARTER, FOLD), bf16),
        compiler_params=PARAMS,
    )(jnp.stack([jnp.int32(offset) for offset in offsets]), *pieces)


STEP = 16


def step_kernel(layout, where_ref, columns_ref, *refs):
    count = 1 + max(array for array, _, _ in layout)
    piece_refs, out_ref, scratch = refs[:count], refs[count], refs[count + 1 :]
    parts, staged, gram, blended, mixed, product, image, out_sems = scratch
    for n, (array, start, rows) in enumerate(layout):
        at = pl.ds(pl.multiple_of(where_ref[2 * n + 1], QUARTER), rows)
        parts[where_ref[2 * n], at, :] = piece_refs[array][start : start + rows, :]
    for folded in range(TILES // 2):
        for row, start in ((folded, 0), (TILES - 1 - folded, TILES - folded)):
            at = slice(row * LANES, (row + 1) * LANES)
            gram[at, row * LANES :] = parts[folded, :, start * LANES : (start + TILES - row) * LANES]
            for column in range(row + 1, TILES, 2):
                wide = min(2, TILES - column) * LANES
                begin = (start + column - row) * LANES
                gram[column * LANES : column * LANES + wide, at] = parts[folded, :, begin : begin + wide].T
    for member in range(MEMBERS):
        blended[:, member * LANES : (member + 1) * LANES] = columns_ref[member]

    def image_of(weights, blocks):
        total = jnp.zeros((8, ROWS), f32)
        for step in range(ROWS // STEP):
            if step % 16 == 0 and step // 16 < len(blocks):
                at = slice(blocks[step // 16] * BLOCK, (blocks[step // 16] + 1) * BLOCK)
                product[:, at] = jnp.dot(blended[...], gram[:, at], preferred_element_type=f32)
            at = slice(step * STEP, (step + 1) * STEP)
            values = gram[at, :].astype(f32)
            if weights is not None:
                values = values * weights[at, :]
            total = total + (values[:8] + values[8:])
        return jnp.sum(total, axis=0, keepdims=True)

    def length_of(values):
        return jnp.sqrt(jnp.sum(values * values) + epsilon_value)

    def stand(values):
        for member in range(MEMBERS):
            at = slice(member * LANES, (member + 1) * LANES)
            image[at, :] = jnp.broadcast_to(values[:, at], (8, LANES)).T[:, :1]

    values = image_of(None, (0, 1))
    stand(values / length_of(values))
    values = image_of(image, (2, 3, 4))
    stand(values / length_of(values))
    values = image_of(image, (5, 6, 7))
    scale = lax.rsqrt(jnp.full((1, 1), length_of(values) + epsilon_value, f32))
    square = scale * scale

    for block in range(8):
        at = slice(block * BLOCK, (block + 1) * BLOCK)
        mixed[:, at] = (second_coef * blended[:, at].astype(f32) + (third_coef * square) * product[:, at]).astype(bf16)
    out_copies = []
    for block in range(8):
        at = slice(block * BLOCK, (block + 1) * BLOCK)
        last = jnp.dot(mixed[...], gram[:, at], preferred_element_type=f32)
        update = (math.sqrt(COLS) * scale) * (first_coef * blended[:, at].astype(f32) + square * last)
        update = update.astype(bf16)
        staged[2 * block] = update[:, :LANES]
        staged[2 * block + 1] = update[:, LANES:]
        at = pl.ds(2 * block, 2)
        out_copies.append(pltpu.make_async_copy(staged.at[at], out_ref.at[at], out_sems.at[block]))
        out_copies[-1].start()
    for copy in out_copies:
        copy.wait()


def newton_step(columns, pieces, layout, where):
    matrix = (MEMBERS, HALF, LANES)
    return pl.pallas_call(
        functools.partial(step_kernel, layout),
        in_specs=[SCALARS, WHOLE] + [WHOLE] * len(pieces),
        out_specs=ANYWHERE,
        out_shape=jax.ShapeDtypeStruct(matrix, bf16),
        scratch_shapes=[
            pltpu.VMEM((CORES * RING, PIECE, FOLD), bf16),
            pltpu.VMEM(matrix, bf16),
            pltpu.VMEM((ROWS, ROWS), bf16),
            pltpu.VMEM((HALF, ROWS), bf16),
            pltpu.VMEM((HALF, ROWS), bf16),
            pltpu.VMEM((HALF, ROWS), f32),
            pltpu.VMEM((ROWS, 1), f32),
            pltpu.SemaphoreType.DMA((8,)),
        ],
        compiler_params=PARAMS,
        cost_estimate=pl.CostEstimate(flops=4 * ROWS * ROWS * HALF, bytes_accessed=8_000_000, transcendentals=0),
    )(where, columns, *pieces)


def spread_kernel(update_ref, out_ref, turned, sems):
    out_copies = []
    for expert in range(EXPERTS):
        turned[expert] = update_ref[expert].T
        out_copies.append(pltpu.make_async_copy(turned.at[expert], out_ref.at[expert], sems.at[expert]))
        out_copies[-1].start()
    for copy in out_copies:
        copy.wait()


def spread(update):
    return pl.pallas_call(
        spread_kernel,
        in_specs=[WHOLE],
        out_specs=ANYWHERE,
        out_shape=jax.ShapeDtypeStruct((EXPERTS, LANES, WIDE), bf16),
        scratch_shapes=[pltpu.VMEM((EXPERTS, LANES, WIDE), bf16), pltpu.SemaphoreType.DMA((EXPERTS,))],
        compiler_params=PARAMS,
    )(update)


def total_of(*terms):
    total = terms[0].astype(f32)
    for term in terms[1:]:
        total = total + term.astype(f32)
    return total


def add(*terms):
    return total_of(*terms).astype(bf16)


def swap_cores(values):
    return lax.ppermute(values, "fsdp", [(i, i ^ 1) for i in range(CORES * RING)])


def shift(values, distance):
    size = CORES * RING
    return lax.ppermute(values, "fsdp", [(i, (i + CORES * distance) % size) for i in range(size)])


def swap_pair(values):
    return lax.ppermute(values, "mat", [(i, i ^ 1) for i in range(MEMBERS)])


def shards(momentum, gradient):
    index = lax.axis_index("fsdp")
    core, place_y = index % CORES, index // CORES
    side = lax.axis_index("mat") % PAIR
    blended = blend(momentum, gradient)
    columns = lax.all_to_all(blended.reshape(MEMBERS, HALF, LANES), "mat", 0, 0)
    new_momentum = momentum_rate * momentum + gradient.astype(f32)

    far, ahead, behind = [(place_y + distance) % RING for distance in (2, 1, 3)]
    slots = jnp.array([3, 1, 0, 2])[(jnp.arange(RING) - place_y) % RING]
    away = gram_pieces(columns, 1 - core, side, slots)
    kept_ring, kept_give, kept_keep = gram_pieces(columns, core, side, slots)
    got_give, got_ring, got_keep = swap_cores(away[1]), swap_cores(away[0]), swap_cores(away[2])

    def round_ring(pieces):
        return [shift(values, distance) for values, distance in zip(pieces, (2, 1, 3))]

    ring_sums = [add(kept_ring[slot], got_ring[slot]) for slot in range(3)]
    partner = swap_pair(add(kept_give, got_give))
    arrived = round_ring(ring_sums)
    first = add(kept_ring[3], got_ring[3], *arrived)
    partner_sums = [add(kept_keep[slot], got_keep[slot], partner[slot]) for slot in range(3)]
    first_got = swap_pair(first)
    arrived = round_ring(partner_sums)
    first = add(first, first_got)
    second = add(kept_keep[3], got_keep[3], partner[3], *arrived)

    second = merge((second, *round_ring([second] * 3)), range(0, PIECE, QUARTER))
    second_other = swap_pair(second)
    pieces, layout, where = [], [], []

    def take(array, rows, chunks, offset):
        for values, half in ((array, core), (swap_cores(array), 1 - core)):
            for n, chunk in enumerate(chunks):
                layout.append((len(pieces), n * rows, rows))
                where.extend([half * RING + chunk, offset])
            pieces.append(values)

    order = [place_y, far, behind, ahead]
    take(first, HALVES, order[:1], 0)
    take(second, QUARTER, order, HALVES + side * QUARTER)
    for values, chunk in zip(round_ring([first] * 3), order[1:]):
        take(values, HALVES, [chunk], 0)
    take(second_other, QUARTER, order, HALVES + (1 - side) * QUARTER)

    update = newton_step(columns, pieces, tuple(layout), jnp.stack(where).astype(jnp.int32))
    returned = lax.all_to_all(update, "mat", 0, 0)
    return new_momentum, spread(returned.reshape(EXPERTS, WIDE, LANES))


def solution(mesh):
    spec = P(None, "mat", "fsdp")
    return jax.shard_map(shards, mesh=mesh, in_specs=(spec, spec), out_specs=(spec, spec), check_vma=False)
```

```python
import functools
import math

import jax
import jax.numpy as jnp
from jax import lax
from jax.experimental import pallas as pl
from jax.experimental.pallas import tpu as pltpu
from jax.sharding import PartitionSpec as P

EXPERTS, ROWS, COLS = 8, 2048, 7168
CORES, RING, PAIR = 2, 4, 2
MEMBERS = 16
LANES = ROWS // MEMBERS
WIDE = COLS // 8
HALF = WIDE // 2
BLOCK = 256
TILES = ROWS // LANES
PIECE = LANES
FOLD = (TILES + 1) * LANES
HALVES = PIECE // PAIR
QUARTER = HALVES // PAIR

momentum_rate = 0.95
first_coef = 3.4445
second_coef = -4.775
third_coef = 2.0315
epsilon_value = 1e-06
f32, bf16 = jnp.float32, jnp.bfloat16
PARAMS = pltpu.CompilerParams(vmem_limit_bytes=50 * 1024 * 1024)
ALL_VMEM = pltpu.CompilerParams(vmem_limit_bytes=60 * 1024 * 1024)
WHOLE = pl.BlockSpec(memory_space=pltpu.VMEM)
ANYWHERE = pl.BlockSpec(memory_space=pl.ANY)
SCALARS = pl.BlockSpec(memory_space=pltpu.SMEM)


def blend_kernel(momentum_ref, gradient_ref, out_ref, momentum, gradient, blended, sems):
    copies = []
    for expert in range(EXPERTS):
        copies.append(pltpu.make_async_copy(momentum_ref.at[expert], momentum.at[expert], sems.at[0, expert]))
        copies.append(pltpu.make_async_copy(gradient_ref.at[expert], gradient.at[expert], sems.at[1, expert]))
    for copy in copies:
        copy.start()
    out_copies = []
    for expert in range(EXPERTS):
        copies[2 * expert].wait()
        copies[2 * expert + 1].wait()
        values = gradient[expert].astype(f32)
        new = momentum_rate * momentum[expert] + values
        blended[expert] = (values + momentum_rate * new).astype(bf16).T
        out_copies.append(pltpu.make_async_copy(blended.at[expert], out_ref.at[expert], sems.at[2, expert]))
        out_copies[-1].start()
    for copy in out_copies:
        copy.wait()


def blend(momentum, gradient):
    return pl.pallas_call(
        blend_kernel,
        in_specs=[ANYWHERE, ANYWHERE],
        out_specs=ANYWHERE,
        out_shape=jax.ShapeDtypeStruct((EXPERTS, WIDE, LANES), bf16),
        scratch_shapes=[
            pltpu.VMEM((EXPERTS, LANES, WIDE), f32),
            pltpu.VMEM((EXPERTS, LANES, WIDE), bf16),
            pltpu.VMEM((EXPERTS, WIDE, LANES), bf16),
            pltpu.SemaphoreType.DMA((3, EXPERTS)),
        ],
        compiler_params=ALL_VMEM,
    )(momentum, gradient)


def gram_kernel(where_ref, columns_ref, ring_ref, give_ref, keep_ref, turned):
    side = where_ref[1]

    def half_of(half):
        folded = range(RING * half, RING * (half + 1))
        rows = sorted([*folded, *(TILES - 1 - row for row in folded)])
        for n, row in enumerate(rows):
            turned[n * LANES : (n + 1) * LANES, :] = columns_ref[row].T
        for column in range(0, TILES, 2):
            used = [row for row in rows if row <= column + 1]
            right = jnp.concatenate([columns_ref[column], columns_ref[column + 1]], axis=1)
            product = jnp.dot(turned[: len(used) * LANES, :], right, preferred_element_type=f32)
            for n, row in enumerate(used):
                begin = LANES if row > column else 0
                values = product[n * LANES : (n + 1) * LANES, begin:].astype(bf16)
                upper, lower = values[HALVES : HALVES + QUARTER], values[HALVES + QUARTER :]
                top = row in folded
                slot = where_ref[2 + (row if top else TILES - 1 - row) - RING * half]
                start = column * LANES + begin + (-row if top else 1) * LANES
                at = slice(start, start + values.shape[1])
                ring_ref[slot, :, at] = values[:HALVES]
                give_ref[slot, :, at] = jnp.where(side == 0, lower, upper)
                keep_ref[slot, :, at] = jnp.where(side == 0, upper, lower)

    for half in range(CORES):
        pl.when(where_ref[0] == half)(functools.partial(half_of, half))


def gram_pieces(columns, half, side, slots):
    where = jnp.concatenate([jnp.stack([half, side]), slots]).astype(jnp.int32)
    shapes = [(RING, HALVES, FOLD), (RING, QUARTER, FOLD), (RING, QUARTER, FOLD)]
    return pl.pallas_call(
        gram_kernel,
        in_specs=[SCALARS, WHOLE],
        out_specs=[WHOLE] * 3,
        out_shape=[jax.ShapeDtypeStruct(shape, bf16) for shape in shapes],
        scratch_shapes=[pltpu.VMEM((ROWS // CORES, HALF), bf16)],
        compiler_params=PARAMS,
        cost_estimate=pl.CostEstimate(flops=16 * PIECE * FOLD * 512, bytes_accessed=8_000_000, transcendentals=0),
    )(where, columns)


def merge_kernel(where_ref, *refs):
    piece_refs, out_ref = refs[:-1], refs[-1]
    for n, piece_ref in enumerate(piece_refs):
        at = pl.ds(pl.multiple_of(where_ref[n], QUARTER), QUARTER)
        out_ref[at, :] = piece_ref[...]


def merge(pieces, offsets):
    count = len(pieces)
    return pl.pallas_call(
        merge_kernel,
        in_specs=[SCALARS] + [WHOLE] * count,
        out_specs=WHOLE,
        out_shape=jax.ShapeDtypeStruct((count * QUARTER, FOLD), bf16),
        compiler_params=PARAMS,
    )(jnp.stack([jnp.int32(offset) for offset in offsets]), *pieces)


STEP = 16


def step_kernel(layout, where_ref, columns_ref, *refs):
    count = 1 + max(array for array, _, _ in layout)
    piece_refs, out_ref, scratch = refs[:count], refs[count], refs[count + 1 :]
    parts, staged, gram, blended, mixed, product, image, out_sems = scratch
    for n, (array, start, rows) in enumerate(layout):
        at = pl.ds(pl.multiple_of(where_ref[2 * n + 1], QUARTER), rows)
        parts[where_ref[2 * n], at, :] = piece_refs[array][start : start + rows, :]
    for folded in range(TILES // 2):
        for row, start in ((folded, 0), (TILES - 1 - folded, TILES - folded)):
            at = slice(row * LANES, (row + 1) * LANES)
            gram[at, row * LANES :] = parts[folded, :, start * LANES : (start + TILES - row) * LANES]
            for column in range(row + 1, TILES, 2):
                wide = min(2, TILES - column) * LANES
                begin = (start + column - row) * LANES
                gram[column * LANES : column * LANES + wide, at] = parts[folded, :, begin : begin + wide].T
    for member in range(MEMBERS):
        blended[:, member * LANES : (member + 1) * LANES] = columns_ref[member]

    def image_of(weights, blocks):
        total = jnp.zeros((8, ROWS), f32)
        for step in range(ROWS // STEP):
            if step % 16 == 0 and step // 16 < len(blocks):
                at = slice(blocks[step // 16] * BLOCK, (blocks[step // 16] + 1) * BLOCK)
                product[:, at] = jnp.dot(blended[...], gram[:, at], preferred_element_type=f32)
            at = slice(step * STEP, (step + 1) * STEP)
            values = gram[at, :].astype(f32)
            if weights is not None:
                values = values * weights[at, :]
            total = total + (values[:8] + values[8:])
        return jnp.sum(total, axis=0, keepdims=True)

    def length_of(values):
        return jnp.sqrt(jnp.sum(values * values) + epsilon_value)

    def stand(values):
        for member in range(MEMBERS):
            at = slice(member * LANES, (member + 1) * LANES)
            image[at, :] = jnp.broadcast_to(values[:, at], (8, LANES)).T[:, :1]

    values = image_of(None, (0, 1))
    stand(values / length_of(values))
    values = image_of(image, (2, 3, 4))
    stand(values / length_of(values))
    values = image_of(image, (5, 6, 7))
    scale = lax.rsqrt(jnp.full((1, 1), length_of(values) + epsilon_value, f32))
    square = scale * scale

    for block in range(8):
        at = slice(block * BLOCK, (block + 1) * BLOCK)
        mixed[:, at] = (second_coef * blended[:, at].astype(f32) + (third_coef * square) * product[:, at]).astype(bf16)
    out_copies = []
    for block in range(8):
        at = slice(block * BLOCK, (block + 1) * BLOCK)
        last = jnp.dot(mixed[...], gram[:, at], preferred_element_type=f32)
        update = (math.sqrt(COLS) * scale) * (first_coef * blended[:, at].astype(f32) + square * last)
        update = update.astype(bf16)
        staged[2 * block] = update[:, :LANES]
        staged[2 * block + 1] = update[:, LANES:]
        at = pl.ds(2 * block, 2)
        out_copies.append(pltpu.make_async_copy(staged.at[at], out_ref.at[at], out_sems.at[block]))
        out_copies[-1].start()
    for copy in out_copies:
        copy.wait()


def newton_step(columns, pieces, layout, where):
    matrix = (MEMBERS, HALF, LANES)
    return pl.pallas_call(
        functools.partial(step_kernel, layout),
        in_specs=[SCALARS, WHOLE] + [WHOLE] * len(pieces),
        out_specs=ANYWHERE,
        out_shape=jax.ShapeDtypeStruct(matrix, bf16),
        scratch_shapes=[
            pltpu.VMEM((CORES * RING, PIECE, FOLD), bf16),
            pltpu.VMEM(matrix, bf16),
            pltpu.VMEM((ROWS, ROWS), bf16),
            pltpu.VMEM((HALF, ROWS), bf16),
            pltpu.VMEM((HALF, ROWS), bf16),
            pltpu.VMEM((HALF, ROWS), f32),
            pltpu.VMEM((ROWS, 1), f32),
            pltpu.SemaphoreType.DMA((8,)),
        ],
        compiler_params=PARAMS,
        cost_estimate=pl.CostEstimate(flops=4 * ROWS * ROWS * HALF, bytes_accessed=8_000_000, transcendentals=0),
    )(where, columns, *pieces)


def spread_kernel(update_ref, out_ref, turned, sems):
    out_copies = []
    for expert in range(EXPERTS):
        turned[expert] = update_ref[expert].T
        out_copies.append(pltpu.make_async_copy(turned.at[expert], out_ref.at[expert], sems.at[expert]))
        out_copies[-1].start()
    for copy in out_copies:
        copy.wait()


def spread(update):
    return pl.pallas_call(
        spread_kernel,
        in_specs=[WHOLE],
        out_specs=ANYWHERE,
        out_shape=jax.ShapeDtypeStruct((EXPERTS, LANES, WIDE), bf16),
        scratch_shapes=[pltpu.VMEM((EXPERTS, LANES, WIDE), bf16), pltpu.SemaphoreType.DMA((EXPERTS,))],
        compiler_params=PARAMS,
    )(update)


def total_of(*terms):
    total = terms[0].astype(f32)
    for term in terms[1:]:
        total = total + term.astype(f32)
    return total


def add(*terms):
    return total_of(*terms).astype(bf16)


def swap_cores(values):
    return lax.ppermute(values, "fsdp", [(i, i ^ 1) for i in range(CORES * RING)])


def shift(values, distance):
    size = CORES * RING
    return lax.ppermute(values, "fsdp", [(i, (i + CORES * distance) % size) for i in range(size)])


def swap_pair(values):
    return lax.ppermute(values, "mat", [(i, i ^ 1) for i in range(MEMBERS)])


def shards(momentum, gradient):
    index = lax.axis_index("fsdp")
    core, place_y = index % CORES, index // CORES
    side = lax.axis_index("mat") % PAIR
    blended = blend(momentum, gradient)
    columns = lax.all_to_all(blended.reshape(MEMBERS, HALF, LANES), "mat", 0, 0)
    new_momentum = momentum_rate * momentum + gradient.astype(f32)

    far, ahead, behind = [(place_y + distance) % RING for distance in (2, 1, 3)]
    slots = jnp.array([3, 1, 0, 2])[(jnp.arange(RING) - place_y) % RING]
    away = gram_pieces(columns, 1 - core, side, slots)
    kept_ring, kept_give, kept_keep = gram_pieces(columns, core, side, slots)
    got_give, got_ring, got_keep = swap_cores(away[1]), swap_cores(away[0]), swap_cores(away[2])

    def round_ring(pieces):
        return [shift(values, distance) for values, distance in zip(pieces, (1, 3, 2))]

    ring_sums = [add(kept_ring[slot], got_ring[slot]) for slot in (1, 2, 0)]
    partner = swap_pair(add(kept_give, got_give))
    arrived = round_ring(ring_sums)
    first = add(kept_ring[3], got_ring[3], *arrived)
    partner_sums = [add(kept_keep[slot], got_keep[slot], partner[slot]) for slot in (1, 2, 0)]
    first_got = swap_pair(first)
    arrived = round_ring(partner_sums)
    first = add(first, first_got)
    second = add(kept_keep[3], got_keep[3], partner[3], *arrived)

    second = merge((second, *round_ring([second] * 3)), range(0, PIECE, QUARTER))
    second_other = swap_pair(second)
    pieces, layout, where = [], [], []

    def take(array, rows, chunks, offset):
        for values, half in ((array, core), (swap_cores(array), 1 - core)):
            for n, chunk in enumerate(chunks):
                layout.append((len(pieces), n * rows, rows))
                where.extend([half * RING + chunk, offset])
            pieces.append(values)

    order = [place_y, behind, ahead, far]
    take(first, HALVES, order[:1], 0)
    take(second, QUARTER, order, HALVES + side * QUARTER)
    for values, chunk in zip(round_ring([first] * 3), order[1:]):
        take(values, HALVES, [chunk], 0)
    take(second_other, QUARTER, order, HALVES + (1 - side) * QUARTER)

    update = newton_step(columns, pieces, tuple(layout), jnp.stack(where).astype(jnp.int32))
    returned = lax.all_to_all(update, "mat", 0, 0)
    return new_momentum, spread(returned.reshape(EXPERTS, WIDE, LANES))


def solution(mesh):
    spec = P(None, "mat", "fsdp")
    return jax.shard_map(shards, mesh=mesh, in_specs=(spec, spec), out_specs=(spec, spec), check_vma=False)
```

```python
import functools
import math

import jax
import jax.numpy as jnp
from jax import lax
from jax.experimental import pallas as pl
from jax.experimental.pallas import tpu as pltpu
from jax.sharding import PartitionSpec as P

EXPERTS, ROWS, COLS = 8, 2048, 7168
CORES, RING, PAIR = 2, 4, 2
MEMBERS = 16
LANES = ROWS // MEMBERS
WIDE = COLS // 8
HALF = WIDE // 2
BLOCK = 256
TILES = ROWS // LANES
PIECE = LANES
FOLD = (TILES + 1) * LANES
HALVES = PIECE // PAIR
QUARTER = HALVES // PAIR

momentum_rate = 0.95
first_coef = 3.4445
second_coef = -4.775
third_coef = 2.0315
epsilon_value = 1e-06
f32, bf16 = jnp.float32, jnp.bfloat16
PARAMS = pltpu.CompilerParams(vmem_limit_bytes=50 * 1024 * 1024)
ALL_VMEM = pltpu.CompilerParams(vmem_limit_bytes=60 * 1024 * 1024)
WHOLE = pl.BlockSpec(memory_space=pltpu.VMEM)
ANYWHERE = pl.BlockSpec(memory_space=pl.ANY)
SCALARS = pl.BlockSpec(memory_space=pltpu.SMEM)


def blend_kernel(momentum_ref, gradient_ref, out_ref, momentum, gradient, blended, sems):
    copies = []
    for expert in range(EXPERTS):
        copies.append(pltpu.make_async_copy(momentum_ref.at[expert], momentum.at[expert], sems.at[0, expert]))
        copies.append(pltpu.make_async_copy(gradient_ref.at[expert], gradient.at[expert], sems.at[1, expert]))
    for copy in copies:
        copy.start()
    out_copies = []
    for expert in range(EXPERTS):
        copies[2 * expert].wait()
        copies[2 * expert + 1].wait()
        values = gradient[expert].astype(f32)
        new = momentum_rate * momentum[expert] + values
        blended[expert] = (values + momentum_rate * new).astype(bf16).T
        out_copies.append(pltpu.make_async_copy(blended.at[expert], out_ref.at[expert], sems.at[2, expert]))
        out_copies[-1].start()
    for copy in out_copies:
        copy.wait()


def blend(momentum, gradient):
    return pl.pallas_call(
        blend_kernel,
        in_specs=[ANYWHERE, ANYWHERE],
        out_specs=ANYWHERE,
        out_shape=jax.ShapeDtypeStruct((EXPERTS, WIDE, LANES), bf16),
        scratch_shapes=[
            pltpu.VMEM((EXPERTS, LANES, WIDE), f32),
            pltpu.VMEM((EXPERTS, LANES, WIDE), bf16),
            pltpu.VMEM((EXPERTS, WIDE, LANES), bf16),
            pltpu.SemaphoreType.DMA((3, EXPERTS)),
        ],
        compiler_params=ALL_VMEM,
    )(momentum, gradient)


def gram_kernel(where_ref, columns_ref, ring_ref, give_ref, keep_ref, turned):
    side = where_ref[1]

    def half_of(half):
        folded = range(RING * half, RING * (half + 1))
        rows = sorted([*folded, *(TILES - 1 - row for row in folded)])
        for n, row in enumerate(rows):
            turned[n * LANES : (n + 1) * LANES, :] = columns_ref[row].T
        for column in range(0, TILES, 2):
            used = [row for row in rows if row <= column + 1]
            right = jnp.concatenate([columns_ref[column], columns_ref[column + 1]], axis=1)
            product = jnp.dot(turned[: len(used) * LANES, :], right, preferred_element_type=f32)
            for n, row in enumerate(used):
                begin = LANES if row > column else 0
                values = product[n * LANES : (n + 1) * LANES, begin:].astype(bf16)
                upper, lower = values[HALVES : HALVES + QUARTER], values[HALVES + QUARTER :]
                top = row in folded
                slot = where_ref[2 + (row if top else TILES - 1 - row) - RING * half]
                start = column * LANES + begin + (-row if top else 1) * LANES
                at = slice(start, start + values.shape[1])
                ring_ref[slot, :, at] = values[:HALVES]
                give_ref[slot, :, at] = jnp.where(side == 0, lower, upper)
                keep_ref[slot, :, at] = jnp.where(side == 0, upper, lower)

    for half in range(CORES):
        pl.when(where_ref[0] == half)(functools.partial(half_of, half))


def gram_pieces(columns, half, side, slots):
    where = jnp.concatenate([jnp.stack([half, side]), slots]).astype(jnp.int32)
    shapes = [(RING, HALVES, FOLD), (RING, QUARTER, FOLD), (RING, QUARTER, FOLD)]
    return pl.pallas_call(
        gram_kernel,
        in_specs=[SCALARS, WHOLE],
        out_specs=[WHOLE] * 3,
        out_shape=[jax.ShapeDtypeStruct(shape, bf16) for shape in shapes],
        scratch_shapes=[pltpu.VMEM((ROWS // CORES, HALF), bf16)],
        compiler_params=PARAMS,
        cost_estimate=pl.CostEstimate(flops=16 * PIECE * FOLD * 512, bytes_accessed=8_000_000, transcendentals=0),
    )(where, columns)


def merge_kernel(where_ref, *refs):
    piece_refs, out_ref = refs[:-1], refs[-1]
    for n, piece_ref in enumerate(piece_refs):
        rows = piece_ref.shape[0]
        out_ref[pl.ds(pl.multiple_of(where_ref[n], QUARTER), rows), :] = piece_ref[...]


def merge(pieces, offsets):
    count, rows = len(pieces), sum(piece.shape[0] for piece in pieces)
    return pl.pallas_call(
        merge_kernel,
        in_specs=[SCALARS] + [WHOLE] * count,
        out_specs=WHOLE,
        out_shape=jax.ShapeDtypeStruct((rows, FOLD), bf16),
        compiler_params=PARAMS,
    )(jnp.stack([jnp.int32(offset) for offset in offsets]), *pieces)


STEP = 16


def step_kernel(layout, where_ref, columns_ref, *refs):
    count = 1 + max(array for array, _, _ in layout)
    piece_refs, out_ref, scratch = refs[:count], refs[count], refs[count + 1 :]
    parts, staged, gram, blended, mixed, product, image, out_sems = scratch
    for n, (array, start, rows) in enumerate(layout):
        at = pl.ds(pl.multiple_of(where_ref[2 * n + 1], QUARTER), rows)
        parts[where_ref[2 * n], at, :] = piece_refs[array][start : start + rows, :]
    for folded in range(TILES // 2):
        for row, start in ((folded, 0), (TILES - 1 - folded, TILES - folded)):
            at = slice(row * LANES, (row + 1) * LANES)
            gram[at, row * LANES :] = parts[folded, :, start * LANES : (start + TILES - row) * LANES]
            for column in range(row + 1, TILES, 2):
                wide = min(2, TILES - column) * LANES
                begin = (start + column - row) * LANES
                gram[column * LANES : column * LANES + wide, at] = parts[folded, :, begin : begin + wide].T
    for member in range(MEMBERS):
        blended[:, member * LANES : (member + 1) * LANES] = columns_ref[member]

    def image_of(weights, blocks):
        total = jnp.zeros((8, ROWS), f32)
        for step in range(ROWS // STEP):
            if step % 16 == 0 and step // 16 < len(blocks):
                at = slice(blocks[step // 16] * BLOCK, (blocks[step // 16] + 1) * BLOCK)
                product[:, at] = jnp.dot(blended[...], gram[:, at], preferred_element_type=f32)
            at = slice(step * STEP, (step + 1) * STEP)
            values = gram[at, :].astype(f32)
            if weights is not None:
                values = values * weights[at, :]
            total = total + (values[:8] + values[8:])
        return jnp.sum(total, axis=0, keepdims=True)

    def length_of(values):
        return jnp.sqrt(jnp.sum(values * values) + epsilon_value)

    def stand(values):
        for member in range(MEMBERS):
            at = slice(member * LANES, (member + 1) * LANES)
            image[at, :] = jnp.broadcast_to(values[:, at], (8, LANES)).T[:, :1]

    values = image_of(None, (0, 1))
    stand(values / length_of(values))
    values = image_of(image, (2, 3, 4))
    stand(values / length_of(values))
    values = image_of(image, (5, 6, 7))
    scale = lax.rsqrt(jnp.full((1, 1), length_of(values) + epsilon_value, f32))
    square = scale * scale

    for block in range(8):
        at = slice(block * BLOCK, (block + 1) * BLOCK)
        mixed[:, at] = (second_coef * blended[:, at].astype(f32) + (third_coef * square) * product[:, at]).astype(bf16)
    out_copies = []
    for block in range(8):
        at = slice(block * BLOCK, (block + 1) * BLOCK)
        last = jnp.dot(mixed[...], gram[:, at], preferred_element_type=f32)
        update = (math.sqrt(COLS) * scale) * (first_coef * blended[:, at].astype(f32) + square * last)
        update = update.astype(bf16)
        staged[2 * block] = update[:, :LANES]
        staged[2 * block + 1] = update[:, LANES:]
        at = pl.ds(2 * block, 2)
        out_copies.append(pltpu.make_async_copy(staged.at[at], out_ref.at[at], out_sems.at[block]))
        out_copies[-1].start()
    for copy in out_copies:
        copy.wait()


def newton_step(columns, pieces, layout, where):
    matrix = (MEMBERS, HALF, LANES)
    return pl.pallas_call(
        functools.partial(step_kernel, layout),
        in_specs=[SCALARS, WHOLE] + [WHOLE] * len(pieces),
        out_specs=ANYWHERE,
        out_shape=jax.ShapeDtypeStruct(matrix, bf16),
        scratch_shapes=[
            pltpu.VMEM((CORES * RING, PIECE, FOLD), bf16),
            pltpu.VMEM(matrix, bf16),
            pltpu.VMEM((ROWS, ROWS), bf16),
            pltpu.VMEM((HALF, ROWS), bf16),
            pltpu.VMEM((HALF, ROWS), bf16),
            pltpu.VMEM((HALF, ROWS), f32),
            pltpu.VMEM((ROWS, 1), f32),
            pltpu.SemaphoreType.DMA((8,)),
        ],
        compiler_params=PARAMS,
        cost_estimate=pl.CostEstimate(flops=4 * ROWS * ROWS * HALF, bytes_accessed=8_000_000, transcendentals=0),
    )(where, columns, *pieces)


def spread_kernel(update_ref, out_ref, turned, sems):
    out_copies = []
    for expert in range(EXPERTS):
        turned[expert] = update_ref[expert].T
        out_copies.append(pltpu.make_async_copy(turned.at[expert], out_ref.at[expert], sems.at[expert]))
        out_copies[-1].start()
    for copy in out_copies:
        copy.wait()


def spread(update):
    return pl.pallas_call(
        spread_kernel,
        in_specs=[WHOLE],
        out_specs=ANYWHERE,
        out_shape=jax.ShapeDtypeStruct((EXPERTS, LANES, WIDE), bf16),
        scratch_shapes=[pltpu.VMEM((EXPERTS, LANES, WIDE), bf16), pltpu.SemaphoreType.DMA((EXPERTS,))],
        compiler_params=PARAMS,
    )(update)


def total_of(*terms):
    total = terms[0].astype(f32)
    for term in terms[1:]:
        total = total + term.astype(f32)
    return total


def add(*terms):
    return total_of(*terms).astype(bf16)


def swap_cores(values):
    return lax.ppermute(values, "fsdp", [(i, i ^ 1) for i in range(CORES * RING)])


def shift(values, distance):
    size = CORES * RING
    return lax.ppermute(values, "fsdp", [(i, (i + CORES * distance) % size) for i in range(size)])


def swap_pair(values):
    return lax.ppermute(values, "mat", [(i, i ^ 1) for i in range(MEMBERS)])


def shards(momentum, gradient):
    index = lax.axis_index("fsdp")
    core, place_y = index % CORES, index // CORES
    side = lax.axis_index("mat") % PAIR
    blended = blend(momentum, gradient)
    columns = lax.all_to_all(blended.reshape(MEMBERS, HALF, LANES), "mat", 0, 0)
    new_momentum = momentum_rate * momentum + gradient.astype(f32)

    far, ahead, behind = [(place_y + distance) % RING for distance in (2, 1, 3)]
    slots = jnp.array([3, 1, 0, 2])[(jnp.arange(RING) - place_y) % RING]
    away = gram_pieces(columns, 1 - core, side, slots)
    kept_ring, kept_give, kept_keep = gram_pieces(columns, core, side, slots)
    got_give, got_ring, got_keep = swap_cores(away[1]), swap_cores(away[0]), swap_cores(away[2])

    def round_ring(pieces):
        return [shift(values, distance) for values, distance in zip(pieces, (1, 3, 2))]

    ring_sums = [add(kept_ring[slot], got_ring[slot]) for slot in (1, 2, 0)]
    partner = swap_pair(add(kept_give, got_give))
    arrived = round_ring(ring_sums)
    first = add(kept_ring[3], got_ring[3], *arrived)
    partner_sums = [add(kept_keep[slot], got_keep[slot], partner[slot]) for slot in (1, 2, 0)]
    first_got = swap_pair(first)
    arrived = round_ring(partner_sums)
    first = add(first, first_got)
    second = add(kept_keep[3], got_keep[3], partner[3], *arrived)

    second = merge((second, *round_ring([second] * 3)), range(0, PIECE, QUARTER))
    second_other = swap_pair(second)
    pieces, layout, where = [], [], []

    def take(array, rows, chunks, offset):
        for values, half in ((array, core), (swap_cores(array), 1 - core)):
            for n, chunk in enumerate(chunks):
                layout.append((len(pieces), n * rows, rows))
                where.extend([half * RING + chunk, offset])
            pieces.append(values)

    order = [place_y, behind, ahead, far]
    take(first, HALVES, order[:1], 0)
    take(second, QUARTER, order, HALVES + side * QUARTER)
    take(merge(round_ring([first] * 3), range(0, 3 * HALVES, HALVES)), HALVES, order[1:], 0)
    take(second_other, QUARTER, order, HALVES + (1 - side) * QUARTER)

    update = newton_step(columns, pieces, tuple(layout), jnp.stack(where).astype(jnp.int32))
    returned = lax.all_to_all(update, "mat", 0, 0)
    return new_momentum, spread(returned.reshape(EXPERTS, WIDE, LANES))


def solution(mesh):
    spec = P(None, "mat", "fsdp")
    return jax.shard_map(shards, mesh=mesh, in_specs=(spec, spec), out_specs=(spec, spec), check_vma=False)
```
